512 devices in a mesh: row: 16 (over z, core), col: 32 (over x, y).
Axes of the slice: x: 4, y: 8, z: 8, core: 2. Of those that a mesh axis runs over, the one named last changes fastest.
Arguments:
- iterate: bfloat16 [4608, 8192], P('row', 'col'), may hold values from -0.046875 to 0.046875
Outputs:
- update: bfloat16 [4608, 8192], P('row', 'col')
The draws below stay inside these ranges and needn't reach their ends.
All inputs are finite; a program needn't handle non-finite values.
Results may differ from the reference program's by a relative error of at most 0.0061.
Values may be sent and summed in bfloat16 or wider, within the bound.
No kernel may reach another device: no remote copies, remote signals or barrier semaphores. Data moves between devices by JAX's collectives and lax.ppermute only.
A program may use at most 64 MiB of HBM per device.

```python
import math
import jax
import jax.numpy as jnp

ROWS = 4608
COLS = 8192


def block_scale(rng, shape, split, low, top_value):
    loudness, own = 1.0, jax.random.fold_in(rng, 6)
    for dim, blocks in split:
        heights = jnp.exp(jax.random.uniform(jax.random.fold_in(own, dim), (blocks,), jnp.float32, low / len(split), top_value / len(split)))
        loudness = loudness * jnp.repeat(heights, shape[dim] // blocks).reshape([-1 if axis == dim else 1 for axis in range(len(shape))])
    return loudness


def noise(own_key, dims, spread, reach, pieces=(), dtype=jnp.bfloat16):
    loudness = block_scale(own_key, dims, pieces, -0.22, 0.18) if pieces else 1.0
    values = jax.random.normal(own_key, dims, jnp.float32) * spread * loudness
    return jnp.minimum(jnp.maximum(values, -reach), reach).astype(dtype)


def setup_inputs(seed: int = 0) -> dict:
    keys = jax.random.split(jax.random.key(seed), 2)
    return {
        "iterate": noise(keys[0], (ROWS, COLS), (2 * COLS) ** -0.5, 0.046875, ((0, 16), (1, 32))),
    }


def reference(iterate):
    gram = jnp.dot(iterate, iterate.T, preferred_element_type=jnp.float32).astype(jnp.bfloat16)
    square = jnp.dot(gram, gram, preferred_element_type=jnp.float32)
    poly = (-4.775 * gram.astype(jnp.float32) + 2.0315 * square).astype(jnp.bfloat16)
    applied = jnp.dot(poly, iterate, preferred_element_type=jnp.float32)
    scale = math.sqrt(COLS)
    return (scale * (3.4445 * iterate.astype(jnp.float32) + applied)).astype(jnp.bfloat16)
```

```python
import math

import jax
import jax.numpy as jnp
from jax import lax
from jax.sharding import Mesh, PartitionSpec as P

COLS = 8192
F32, BF16 = jnp.float32, jnp.bfloat16


def exchange(chunks, axis):
    return lax.all_to_all(chunks, axis, 0, 0)


def gather(block, axis):
    return exchange(jnp.broadcast_to(block, (lax.axis_size(axis), *block.shape)), axis)


def reduce_scatter(chunks, axis):
    return jnp.sum(exchange(chunks, axis).astype(F32), 0)


def swap_cores(block):
    return lax.ppermute(block, "core", [(0, 1), (1, 0)])


def on_device(own):
    rows, cols = own.shape
    nx, ny, nz = (lax.axis_size(a) for a in "xyz")
    quarter = rows // nx
    core = lax.axis_index("core")

    wide = gather(own, "x")
    wide_peer = swap_cores(wide)
    share = lax.dynamic_slice_in_dim(wide, lax.axis_index("x") * quarter, quarter, 1)
    panel = gather(share, "z")

    def gram_of(mine):
        return jnp.einsum("xrc,zxsc->rzs", mine, panel, preferred_element_type=F32)

    partial = jnp.concatenate([gram_of(wide), gram_of(wide_peer)], 0).astype(BF16)
    partial = partial.reshape(ny, 2 * rows // ny, nz * quarter)
    gram = gather(reduce_scatter(partial, "y").astype(BF16), "y")
    gram = gram.reshape(2, rows, nz, quarter)

    def applied(right):
        mine = jnp.einsum("rzs,zxsc->xrc", gram[0], right, preferred_element_type=F32)
        peer = jnp.einsum("rzs,zxsc->xrc", gram[1], right, preferred_element_type=F32)
        return mine + swap_cores(peer.astype(BF16)).astype(F32)

    first = applied(panel).reshape(nx, nx, quarter, cols).swapaxes(0, 1).astype(BF16)
    first = reduce_scatter(first, "x")
    inner = (-4.775 * share.astype(F32) + 2.0315 * first).astype(BF16)
    second = reduce_scatter(applied(gather(inner, "z")).astype(BF16), "x")
    scale = math.sqrt(COLS)
    return (scale * (3.4445 * own.astype(F32) + second)).astype(BF16)


def solution(mesh):
    fine = Mesh(mesh.devices.reshape(8, 2, 4, 8), ("z", "core", "x", "y"))
    placed = P(("z", "core"), ("x", "y"))
    return jax.shard_map(
        on_device, mesh=fine, in_specs=placed, out_specs=placed, check_vma=False
    )
```

```python
import math

import jax
import jax.numpy as jnp
from jax import lax
from jax.sharding import Mesh, PartitionSpec as P

COLS = 8192
F32, BF16 = jnp.float32, jnp.bfloat16


def exchange(chunks, axis):
    return lax.all_to_all(chunks, axis, 0, 0)


def gather(block, axis):
    return exchange(jnp.broadcast_to(block, (lax.axis_size(axis), *block.shape)), axis)


def reduce_scatter(chunks, axis):
    parts = exchange(chunks, axis)
    return sum(parts[i].astype(F32) for i in range(parts.shape[0]))


def swap_cores(block):
    return lax.ppermute(block, "core", [(0, 1), (1, 0)])


def on_device(own):
    rows, cols = own.shape
    nx, ny, nz = (lax.axis_size(a) for a in "xyz")
    quarter = rows // nx

    split = own.reshape(1, nx, quarter, cols)
    spread = jnp.broadcast_to(split, (nz, nx, quarter, cols)).reshape(nz * nx, quarter, cols)
    panel = exchange(spread, ("z", "x")).reshape(nz, nx, quarter, cols)
    here = lax.axis_index("x")
    wide = jnp.zeros((nx, rows, cols), BF16)
    for hop in range(nx):
        moves = [(i, (i + hop) % nx) for i in range(nx)]
        block = lax.ppermute(own, "x", moves) if hop else own
        wide = lax.dynamic_update_index_in_dim(wide, block, lax.rem(here + (nx - hop), nx), 0)
    share = lax.dynamic_slice_in_dim(wide, here * quarter, quarter, 1)

    def both(mine):
        return mine, swap_cores(mine)

    panels = both(panel)
    partial = [
        jnp.einsum("xrc,zxsc->rzs", wide, p, preferred_element_type=F32)
        .astype(BF16)
        .reshape(rows, nz * quarter)
        for p in panels
    ]
    partial = jnp.concatenate(partial, 1).reshape(ny, rows // ny, 2 * nz * quarter)
    gram = gather(reduce_scatter(partial, "y").astype(BF16), "y")
    gram = gram.reshape(rows, 2, nz, quarter)

    def applied(right):
        return sum(
            jnp.einsum("rzs,zxsc->xrc", gram[:, i], p, preferred_element_type=F32)
            for i, p in enumerate(right)
        ).astype(BF16)

    first = applied(panels).reshape(nx, nx, quarter, cols).swapaxes(0, 1)
    first = reduce_scatter(first, "x")
    inner = (-4.775 * share.astype(F32) + 2.0315 * first).astype(BF16)
    second = reduce_scatter(applied(both(gather(inner, "z"))), "x")
    scale = math.sqrt(COLS)
    return (scale * (3.4445 * own.astype(F32) + second)).astype(BF16)


def solution(mesh):
    fine = Mesh(mesh.devices.reshape(8, 2, 4, 8), ("z", "core", "x", "y"))
    placed = P(("z", "core"), ("x", "y"))
    return jax.shard_map(
        on_device, mesh=fine, in_specs=placed, out_specs=placed, check_vma=False
    )
```

```python
import math

import jax
import jax.numpy as jnp
from jax import lax
from jax.sharding import Mesh, PartitionSpec as P

COLS = 8192
SHIFT = 2.0
F32, BF16 = jnp.float32, jnp.bfloat16


def exchange(chunks, axis):
    return lax.all_to_all(chunks, axis, 0, 0)


def gather(block, axis):
    return exchange(jnp.broadcast_to(block, (lax.axis_size(axis), *block.shape)), axis)


def reduce_scatter(chunks, axis):
    parts = exchange(chunks, axis)
    return sum(parts[i].astype(F32) for i in range(parts.shape[0]))


def swap_cores(block):
    return lax.ppermute(block, "core", [(0, 1), (1, 0)])


def in_columns(block, parts):
    return block.reshape(block.shape[0], parts, -1).swapaxes(0, 1)


def on_device(own):
    rows, cols = own.shape
    nx, ny, nz = (lax.axis_size(a) for a in "xyz")
    quarter = rows // nx
    depth = nz * quarter
    here = lax.axis_index("x")

    split = own.reshape(1, nx, quarter, cols)
    spread = jnp.broadcast_to(split, (nz, nx, quarter, cols)).reshape(nz * nx, quarter, cols)
    panel = exchange(spread, ("z", "x")).reshape(nz, nx, quarter, cols)
    panel = jnp.concatenate([panel[:, x].reshape(depth, cols) for x in range(nx)], 1)
    blocks = [own]
    for hop in range(1, nx):
        blocks.append(lax.ppermute(own, "x", [(i, (i + hop) % nx) for i in range(nx)]))
    order = [lax.rem(here + (nx - x), nx) for x in range(nx)]
    wide = jnp.concatenate([lax.select_n(hop, *blocks) for hop in order], 1)
    share = lax.dynamic_slice_in_dim(wide, here * quarter, quarter, 0)

    left = jnp.concatenate([wide, swap_cores(wide)], 0)
    partial = lax.dot_general(left, panel, (((1,), (1,)), ((), ())), preferred_element_type=F32)
    partial = partial.astype(BF16).reshape(ny, 2 * rows // ny, depth)
    gram = gather(reduce_scatter(partial, "y").astype(BF16), "y").reshape(2 * rows, depth)

    def applied(right):
        peer = jnp.dot(gram[rows:], right, preferred_element_type=F32).astype(BF16)
        mine = jnp.dot(gram[:rows], right, preferred_element_type=F32)
        return mine + swap_cores(peer).astype(F32)

    first = reduce_scatter(applied(panel).astype(BF16).reshape(nx, quarter, nx * cols), "x")
    inner = (-4.775 * share.astype(F32) + 2.0315 * first).astype(BF16)
    right = gather(inner, "z").reshape(depth, nx * cols)
    mask = jnp.where(jnp.arange(nx) == here, SHIFT, 0.0)
    known = (mask[:, None, None] * share.astype(F32)).reshape(rows, nx * cols)
    second = reduce_scatter(in_columns((applied(right) + known).astype(BF16), nx), "x")
    scale = math.sqrt(COLS)
    return (scale * ((3.4445 - SHIFT) * own.astype(F32) + second)).astype(BF16)


def solution(mesh):
    fine = Mesh(mesh.devices.reshape(8, 2, 4, 8), ("z", "core", "x", "y"))
    placed = P(("z", "core"), ("x", "y"))
    return jax.shard_map(
        on_device, mesh=fine, in_specs=placed, out_specs=placed, check_vma=False
    )
```

```python
import math

import jax
import jax.numpy as jnp
from jax import lax
from jax.sharding import Mesh, PartitionSpec as P

COLS = 8192
SHIFT = 2.0
F32, BF16 = jnp.float32, jnp.bfloat16


def exchange(chunks, axis):
    return lax.all_to_all(chunks, axis, 0, 0)


def gather(block, axis):
    return exchange(jnp.broadcast_to(block, (lax.axis_size(axis), *block.shape)), axis)


def reduce_scatter(chunks, axis):
    parts = exchange(chunks, axis)
    return sum(parts[i].astype(F32) for i in range(parts.shape[0]))


def swap_cores(block):
    return lax.ppermute(block, "core", [(0, 1), (1, 0)])


def by_column(blocks):
    n, nx, rows, cols = blocks.shape
    return blocks.swapaxes(0, 1).reshape(nx, n * rows, cols)


def on_device(own):
    rows, cols = own.shape
    nx, ny, nz = (lax.axis_size(a) for a in "xyz")
    quarter = rows // nx
    depth = nz * quarter
    here = lax.axis_index("x")

    split = own.reshape(1, nx, quarter, cols)
    spread = jnp.broadcast_to(split, (nz, nx, quarter, cols)).reshape(nz * nx, quarter, cols)
    panel = by_column(exchange(spread, ("z", "x")).reshape(nz, nx, quarter, cols))
    blocks = [own]
    for hop in range(1, nx):
        blocks.append(lax.ppermute(own, "x", [(i, (i + hop) % nx) for i in range(nx)]))
    order = [lax.rem(here + (nx - x), nx) for x in range(nx)]
    wide = jnp.stack([lax.select_n(hop, *blocks) for hop in order])
    share = lax.dynamic_slice_in_dim(wide, here * quarter, quarter, 1)

    left = jnp.concatenate([wide, swap_cores(wide)], 1)
    partial = jnp.einsum("xrc,xjc->rj", left, panel, preferred_element_type=F32)
    partial = partial.astype(BF16).reshape(ny, 2 * rows // ny, depth)
    partial, share = lax.optimization_barrier((partial, share))
    gram = gather(reduce_scatter(partial, "y").astype(BF16), "y").reshape(2 * rows, depth)

    def times(left, right):
        return jnp.einsum("rj,xjc->xrc", left, right, preferred_element_type=F32)

    def applied(right):
        peer = swap_cores(times(gram[rows:], right).astype(BF16))
        return lax.optimization_barrier(times(gram[:rows], right)) + peer.astype(F32)

    first = applied(panel).astype(BF16).reshape(nx, nx, quarter, cols).swapaxes(0, 1)
    first = reduce_scatter(first, "x")
    inner = (-4.775 * share.astype(F32) + 2.0315 * first).astype(BF16)
    right = by_column(gather(inner, "z"))
    mask = jnp.where(jnp.arange(nx) == here, SHIFT, 0.0)[:, None, None]
    known = (mask * share[:, None].astype(F32)).reshape(nx, rows, cols)
    second = reduce_scatter((applied(right) + known).astype(BF16), "x")
    scale = math.sqrt(COLS)
    return (scale * ((3.4445 - SHIFT) * own.astype(F32) + second)).astype(BF16)


def solution(mesh):
    fine = Mesh(mesh.devices.reshape(8, 2, 4, 8), ("z", "core", "x", "y"))
    placed = P(("z", "core"), ("x", "y"))
    return jax.shard_map(
        on_device, mesh=fine, in_specs=placed, out_specs=placed, check_vma=False
    )
```

```python
import math

import jax
import jax.numpy as jnp
from jax import lax
from jax.sharding import Mesh, PartitionSpec as P

COLS = 8192
F32, BF16 = jnp.float32, jnp.bfloat16


def exchange(chunks, axis):
    return lax.all_to_all(chunks, axis, 0, 0)


def gather(block, axis):
    return exchange(jnp.broadcast_to(block, (lax.axis_size(axis), *block.shape)), axis)


def reduce_scatter(chunks, axis):
    parts = exchange(chunks, axis)
    return sum(parts[i].astype(F32) for i in range(parts.shape[0]))


def swap_cores(block):
    return lax.ppermute(block, "core", [(0, 1), (1, 0)])


def by_column(blocks):
    n, nx, rows, cols = blocks.shape
    return blocks.swapaxes(0, 1).reshape(nx, n * rows, cols)


def on_device(own):
    rows, cols = own.shape
    nx, ny, nz = (lax.axis_size(a) for a in "xyz")
    quarter = rows // nx
    depth = nz * quarter
    here = lax.axis_index("x")

    def shift_x(block, hop):
        return lax.ppermute(block, "x", [(i, (i + hop) % nx) for i in range(nx)])

    chunks = jnp.broadcast_to(own.reshape(nx, quarter, cols), (nz, nx, quarter, cols))
    chunks = exchange(chunks.reshape(nz * nx, quarter, cols), ("z", "x"))
    panel = by_column(chunks.reshape(nz, nx, quarter, cols))
    blocks = [own] + [shift_x(own, hop) for hop in range(1, nx)]
    order = [lax.rem(here + (nx - x), nx) for x in range(nx)]
    wide = jnp.stack([lax.select_n(hop, *blocks) for hop in order])

    left = jnp.concatenate([wide, swap_cores(wide)], 1)
    partial = jnp.einsum("xrc,xjc->rj", left, panel, preferred_element_type=F32)
    partial = partial.astype(BF16).reshape(ny, 2 * rows // ny, depth)
    gram = gather(reduce_scatter(partial, "y").astype(BF16), "y").reshape(2 * rows, depth)

    def times(left, right):
        return jnp.einsum("rj,xjc->xrc", left, right, preferred_element_type=F32)

    def applied(right):
        peer = swap_cores(times(gram[rows:], right).astype(BF16))
        return lax.optimization_barrier(times(gram[:rows], right)) + peer.astype(F32)

    first = reduce_scatter(applied(panel).astype(BF16), "x")
    inner = (-4.775 * own.astype(F32) + 2.0315 * first).astype(BF16).reshape(nx, quarter, cols)
    inner, gram = lax.optimization_barrier((inner, gram))
    right = by_column(gather(inner, "z"))
    top, bottom = gram[:rows], gram[rows:]
    above_top, below_bottom = shift_x(top, -1), shift_x(bottom, 1)
    above_bottom, below_top = shift_x(bottom, -1), shift_x(top, 1)
    far_top, far_bottom = shift_x(above_top, -1), shift_x(below_bottom, 1)
    tops = jnp.stack([lax.select_n(hop, top, below_top, far_top, above_top) for hop in order])
    bottoms = jnp.stack([lax.select_n(hop, bottom, below_bottom, far_bottom, above_bottom) for hop in order])

    def with_all(left):
        return jnp.einsum("xrj,xjc->rc", left, right, preferred_element_type=F32)

    other = swap_cores(with_all(bottoms))
    second = lax.optimization_barrier(with_all(tops)) + other
    scale = math.sqrt(COLS)
    return (scale * (3.4445 * own.astype(F32) + second)).astype(BF16)


def solution(mesh):
    fine = Mesh(mesh.devices.reshape(8, 2, 4, 8), ("z", "core", "x", "y"))
    placed = P(("z", "core"), ("x", "y"))
    return jax.shard_map(
        on_device, mesh=fine, in_specs=placed, out_specs=placed, check_vma=False
    )
```

```python
import math

import jax
import jax.numpy as jnp
from jax import lax
from jax.experimental import pallas as pl
from jax.experimental.pallas import tpu as pltpu
from jax.sharding import Mesh, PartitionSpec as P

COLS = 8192
F32, BF16 = jnp.float32, jnp.bfloat16


def exchange(chunks, axis):
    return lax.all_to_all(chunks, axis, 0, 0)


def gather(block, axis):
    return exchange(jnp.broadcast_to(block, (lax.axis_size(axis), *block.shape)), axis)


def reduce_scatter(chunks, axis):
    parts = exchange(chunks, axis)
    return sum(parts[i].astype(F32) for i in range(parts.shape[0]))


def swap_cores(block):
    return lax.ppermute(block, "core", [(0, 1), (1, 0)])


def by_column(blocks):
    n, nx, rows, cols = blocks.shape
    return blocks.swapaxes(0, 1).reshape(nx, n * rows, cols)


def product_kernel(right, *refs):
    *blocks, out = refs
    nx = right.shape[0]
    here = lax.axis_index("x")
    out[...] = sum(
        jnp.dot(block[...], right[lax.rem(here + (nx - hop), nx)], preferred_element_type=F32)
        for hop, block in enumerate(blocks)
    )


def product(right, *blocks):
    rows, depth = blocks[0].shape
    cols = right.shape[2]
    size = 2 * rows * depth * cols * len(blocks)
    moved = 2 * right.size + 2 * rows * depth * len(blocks) + 4 * rows * cols
    return pl.pallas_call(
        product_kernel,
        out_shape=jax.ShapeDtypeStruct((rows, cols), F32),
        in_specs=[pl.BlockSpec(memory_space=pltpu.VMEM)] * (1 + len(blocks)),
        out_specs=pl.BlockSpec(memory_space=pltpu.VMEM),
        compiler_params=pltpu.CompilerParams(vmem_limit_bytes=16 << 20),
        cost_estimate=pl.CostEstimate(flops=size, bytes_accessed=moved, transcendentals=0),
    )(right, *blocks)


def on_device(own):
    rows, cols = own.shape
    nx, ny, nz = (lax.axis_size(a) for a in "xyz")
    quarter = rows // nx
    depth = nz * quarter
    here = lax.axis_index("x")

    def shift_x(block, hop):
        return lax.ppermute(block, "x", [(i, (i + hop) % nx) for i in range(nx)])

    chunks = jnp.broadcast_to(own.reshape(nx, quarter, cols), (nz, nx, quarter, cols))
    chunks = exchange(chunks.reshape(nz * nx, quarter, cols), ("z", "x"))
    panel = by_column(chunks.reshape(nz, nx, quarter, cols))
    blocks = [own] + [shift_x(own, hop) for hop in range(1, nx)]
    order = [lax.rem(here + (nx - hop), nx) for hop in range(nx)]
    wide = jnp.stack([lax.select_n(hop, *blocks) for hop in order])

    left = jnp.concatenate([wide, swap_cores(wide)], 1)
    partial = jnp.einsum("xrc,xjc->rj", left, panel, preferred_element_type=F32)
    partial = partial.astype(BF16).reshape(ny, 2 * rows // ny, depth)
    gram = gather(reduce_scatter(partial, "y").astype(BF16), "y").reshape(2 * rows, depth)

    def times(left, right):
        return jnp.einsum("rj,xjc->xrc", left, right, preferred_element_type=F32)

    def applied(right):
        peer = swap_cores(times(gram[rows:], right).astype(BF16))
        return lax.optimization_barrier(times(gram[:rows], right)) + peer.astype(F32)

    first = reduce_scatter(applied(panel).astype(BF16), "x")
    inner = (-4.775 * own.astype(F32) + 2.0315 * first).astype(BF16).reshape(nx, quarter, cols)
    inner, gram = lax.optimization_barrier((inner, gram))
    right = by_column(gather(inner, "z"))
    top, bottom = gram[:rows], gram[rows:]
    above_top, below_bottom = shift_x(top, -1), shift_x(bottom, 1)
    above_bottom, below_top = shift_x(bottom, -1), shift_x(top, 1)
    far_top, far_bottom = shift_x(above_top, -1), shift_x(below_bottom, 1)
    other = swap_cores(product(right, bottom, below_bottom, far_bottom, above_bottom))
    second = product(right, top, below_top, far_top, above_top) + other
    scale = math.sqrt(COLS)
    return (scale * (3.4445 * own.astype(F32) + second)).astype(BF16)


def solution(mesh):
    fine = Mesh(mesh.devices.reshape(8, 2, 4, 8), ("z", "core", "x", "y"))
    placed = P(("z", "core"), ("x", "y"))
    return jax.shard_map(
        on_device, mesh=fine, in_specs=placed, out_specs=placed, check_vma=False
    )
```

```python
import math

import jax
import jax.numpy as jnp
from jax import lax
from jax.experimental import pallas as pl
from jax.experimental.pallas import tpu as pltpu
from jax.sharding import Mesh, PartitionSpec as P

COLS = 8192
F32, BF16 = jnp.float32, jnp.bfloat16


def exchange(chunks, axis):
    return lax.all_to_all(chunks, axis, 0, 0)


def gather(block, axis):
    return exchange(jnp.broadcast_to(block, (lax.axis_size(axis), *block.shape)), axis)


def reduce_scatter(chunks, axis):
    parts = exchange(chunks, axis)
    return sum(parts[i].astype(F32) for i in range(parts.shape[0]))


def swap_cores(block):
    return lax.ppermute(block, "core", [(0, 1), (1, 0)])


def by_column(blocks):
    n, nx, rows, cols = blocks.shape
    return blocks.swapaxes(0, 1).reshape(nx, n * rows, cols)


def product_kernel(right, *refs):
    *blocks, out = refs
    nx = right.shape[0]
    here = lax.axis_index("x")
    out[...] = sum(
        jnp.dot(block[...], right[lax.rem(here + (nx - hop), nx)], preferred_element_type=F32)
        for hop, block in enumerate(blocks)
    )


def product(right, *blocks):
    rows, depth = blocks[0].shape
    cols = right.shape[2]
    size = 2 * rows * depth * cols * len(blocks)
    moved = 2 * right.size + 2 * rows * depth * len(blocks) + 4 * rows * cols
    return pl.pallas_call(
        product_kernel,
        out_shape=jax.ShapeDtypeStruct((rows, cols), F32),
        in_specs=[pl.BlockSpec(memory_space=pltpu.VMEM)] * (1 + len(blocks)),
        out_specs=pl.BlockSpec(memory_space=pltpu.VMEM),
        compiler_params=pltpu.CompilerParams(vmem_limit_bytes=16 << 20),
        cost_estimate=pl.CostEstimate(flops=size, bytes_accessed=moved, transcendentals=0),
    )(right, *blocks)


def on_device(own):
    rows, cols = own.shape
    nx, ny, nz = (lax.axis_size(a) for a in "xyz")
    quarter = rows // nx
    depth = nz * quarter
    here = lax.axis_index("x")

    def shift_x(block, hop):
        return lax.ppermute(block, "x", [(i, (i + hop) % nx) for i in range(nx)])

    chunks = jnp.broadcast_to(own.reshape(nx, quarter, cols), (nz, nx, quarter, cols))
    chunks = exchange(chunks.reshape(nz * nx, quarter, cols), ("z", "x"))
    panel = by_column(chunks.reshape(nz, nx, quarter, cols))
    blocks = [own] + [shift_x(own, hop) for hop in range(1, nx)]
    order = [lax.rem(here + (nx - hop), nx) for hop in range(nx)]
    wide = jnp.stack([lax.select_n(hop, *blocks) for hop in order])

    left = jnp.concatenate([wide, swap_cores(wide)], 1)
    partial = jnp.einsum("xrc,xjc->rj", left, panel, preferred_element_type=F32)
    partial = partial.astype(BF16).reshape(ny, 2 * rows // ny, depth)
    gram = gather(reduce_scatter(partial, "y").astype(BF16), "y").reshape(2 * rows, depth)
    top, bottom = gram[:rows], gram[rows:]

    def times(left, right):
        return jnp.einsum("rj,xjc->xrc", left, right, preferred_element_type=F32)

    def applied(right):
        peer = swap_cores(times(bottom, right).astype(BF16))
        return lax.optimization_barrier(times(top, right)) + peer.astype(F32)

    first = reduce_scatter(applied(panel).astype(BF16), "x")
    inner = (-4.775 * own.astype(F32) + 2.0315 * first).astype(BF16).reshape(nx, quarter, cols)
    inner, top, bottom = lax.optimization_barrier((inner, top, bottom))
    right = by_column(gather(inner, "z"))
    above_top, below_bottom = shift_x(top, -1), shift_x(bottom, 1)
    above_bottom, below_top = shift_x(bottom, -1), shift_x(top, 1)
    far_top, far_bottom = shift_x(above_top, -1), shift_x(below_bottom, 1)
    other = swap_cores(product(right, bottom, below_bottom, far_bottom, above_bottom))
    second = product(right, top, below_top, far_top, above_top) + other
    scale = math.sqrt(COLS)
    return (scale * (3.4445 * own.astype(F32) + second)).astype(BF16)


def solution(mesh):
    fine = Mesh(mesh.devices.reshape(8, 2, 4, 8), ("z", "core", "x", "y"))
    placed = P(("z", "core"), ("x", "y"))
    return jax.shard_map(
        on_device, mesh=fine, in_specs=placed, out_specs=placed, check_vma=False
    )
```

```python
import math

import jax
import jax.numpy as jnp
from jax import lax
from jax.experimental import pallas as pl
from jax.experimental.pallas import tpu as pltpu
from jax.sharding import Mesh, PartitionSpec as P

COLS = 8192
F32, BF16 = jnp.float32, jnp.bfloat16


def exchange(chunks, axis):
    return lax.all_to_all(chunks, axis, 0, 0)


def gather(block, axis):
    return exchange(jnp.broadcast_to(block, (lax.axis_size(axis), *block.shape)), axis)


def reduce_scatter(chunks, axis):
    parts = exchange(chunks, axis)
    return sum(parts[i].astype(F32) for i in range(parts.shape[0]))


def swap_cores(block):
    return lax.ppermute(block, "core", [(0, 1), (1, 0)])


def by_column(blocks):
    n, nx, rows, cols = blocks.shape
    return blocks.swapaxes(0, 1).reshape(nx, n * rows, cols)


def product_kernel(blocks, right, out):
    nx = right.shape[0]
    here = lax.axis_index("x")
    out[...] = sum(
        jnp.dot(blocks[hop], right[lax.rem(here + (nx - hop), nx)], preferred_element_type=F32)
        for hop in range(nx)
    )


def product(blocks, right):
    _, rows, _ = blocks.shape
    cols = right.shape[2]
    return pl.pallas_call(
        product_kernel,
        out_shape=jax.ShapeDtypeStruct((rows, cols), F32),
        in_specs=[pl.BlockSpec(memory_space=pltpu.VMEM)] * 2,
        out_specs=pl.BlockSpec(memory_space=pltpu.VMEM),
        compiler_params=pltpu.CompilerParams(vmem_limit_bytes=16 << 20),
        cost_estimate=pl.CostEstimate(
            flops=2 * blocks.size * cols,
            bytes_accessed=2 * right.size + 2 * blocks.size + 4 * rows * cols,
            transcendentals=0,
        ),
    )(blocks, right)


def on_device(own):
    rows, cols = own.shape
    nx, ny, nz = (lax.axis_size(a) for a in "xyz")
    quarter = rows // nx
    depth = nz * quarter
    here = lax.axis_index("x")

    def shift_x(block, hop):
        return lax.ppermute(block, "x", [(i, (i + hop) % nx) for i in range(nx)])

    chunks = jnp.broadcast_to(own.reshape(nx, quarter, cols), (nz, nx, quarter, cols))
    chunks = exchange(chunks.reshape(nz * nx, quarter, cols), ("z", "x"))
    panel = by_column(chunks.reshape(nz, nx, quarter, cols))
    blocks = [own] + [shift_x(own, hop) for hop in range(1, nx)]
    order = [lax.rem(here + (nx - hop), nx) for hop in range(nx)]
    wide = jnp.stack([lax.select_n(hop, *blocks) for hop in order])

    left = jnp.concatenate([wide, swap_cores(wide)], 1)
    partial = jnp.einsum("xrc,xjc->rj", left, panel, preferred_element_type=F32)
    partial = partial.astype(BF16).reshape(ny, 2 * rows // ny, depth)
    gram = gather(reduce_scatter(partial, "y").astype(BF16), "y").reshape(2 * rows, depth)
    top, bottom = gram[:rows], gram[rows:]

    def times(left, right):
        return jnp.einsum("rj,xjc->xrc", left, right, preferred_element_type=F32)

    def applied(right):
        peer = swap_cores(times(bottom, right).astype(BF16))
        return lax.optimization_barrier(times(top, right)) + peer.astype(F32)

    first = reduce_scatter(applied(panel).astype(BF16), "x")
    inner = (-4.775 * own.astype(F32) + 2.0315 * first).astype(BF16).reshape(nx, quarter, cols)
    inner, top, bottom = lax.optimization_barrier((inner, top, bottom))
    right = by_column(gather(inner, "z"))
    above_top, below_bottom = shift_x(top, -1), shift_x(bottom, 1)
    above_bottom, below_top = shift_x(bottom, -1), shift_x(top, 1)
    far_top, far_bottom = shift_x(above_top, -1), shift_x(below_bottom, 1)
    bottoms = jnp.stack([bottom, below_bottom, far_bottom, above_bottom])
    other = swap_cores(product(bottoms, right))
    tops = jnp.stack([top, below_top, far_top, above_top])
    second = product(tops, right) + other
    scale = math.sqrt(COLS)
    return (scale * (3.4445 * own.astype(F32) + second)).astype(BF16)


def solution(mesh):
    fine = Mesh(mesh.devices.reshape(8, 2, 4, 8), ("z", "core", "x", "y"))
    placed = P(("z", "core"), ("x", "y"))
    return jax.shard_map(
        on_device, mesh=fine, in_specs=placed, out_specs=placed, check_vma=False
    )
```

```python
import math

import jax
import jax.numpy as jnp
from jax import lax
from jax.experimental import pallas as pl
from jax.experimental.pallas import tpu as pltpu
from jax.sharding import Mesh, PartitionSpec as P

COLS = 8192
F32, BF16 = jnp.float32, jnp.bfloat16


def exchange(chunks, axis):
    return lax.all_to_all(chunks, axis, 0, 0)


def gather(block, axis):
    return exchange(jnp.broadcast_to(block, (lax.axis_size(axis), *block.shape)), axis)


def reduce_scatter(chunks, axis):
    parts = exchange(chunks, axis)
    return sum(parts[i].astype(F32) for i in range(parts.shape[0]))


def swap_cores(block):
    return lax.ppermute(block, "core", [(0, 1), (1, 0)])


def by_column(blocks):
    n, nx, rows, cols = blocks.shape
    return blocks.swapaxes(0, 1).reshape(nx, n * rows, cols)


def product_kernel(blocks, right, out):
    nx = right.shape[0]
    here = lax.axis_index("x")
    out[...] = sum(
        jnp.dot(blocks[hop], right[lax.rem(here + (nx - hop), nx)], preferred_element_type=F32)
        for hop in range(nx)
    )


def product(blocks, right):
    _, rows, _ = blocks.shape
    cols = right.shape[2]
    return pl.pallas_call(
        product_kernel,
        out_shape=jax.ShapeDtypeStruct((rows, cols), F32),
        in_specs=[pl.BlockSpec(memory_space=pltpu.VMEM)] * 2,
        out_specs=pl.BlockSpec(memory_space=pltpu.VMEM),
        compiler_params=pltpu.CompilerParams(vmem_limit_bytes=16 << 20),
        cost_estimate=pl.CostEstimate(
            flops=2 * blocks.size * cols,
            bytes_accessed=2 * right.size + 2 * blocks.size + 4 * rows * cols,
            transcendentals=0,
        ),
    )(blocks, right)


LANES = 128


def gram_kernel(left, right, out):
    nx, rows, _ = left.shape
    total = sum(
        lax.dot_general(left[i], right[i], (((1,), (1,)), ((), ())), preferred_element_type=F32)
        for i in range(nx)
    ).astype(BF16)
    parts, half = out.shape[0], rows // 2
    share = out.shape[1] - half
    for part in range(parts):
        tile, side = part // 2, part % 2
        out[part, :half, :] = total[side * half : (side + 1) * half, tile * LANES : (tile + 1) * LANES]
    last = parts // 2 * LANES
    tail = jnp.concatenate([total[:half, last:], total[half:, last:]], 1)
    for part in range(parts):
        if part * share < half:
            out[part, half:, :] = tail[part * share : (part + 1) * share]
        else:
            out[part, half:, :] = jnp.zeros((share, LANES), BF16)


def packed_gram(left, right, parts):
    nx, rows, cols = left.shape
    share = 48
    return pl.pallas_call(
        gram_kernel,
        out_shape=jax.ShapeDtypeStruct((parts, rows // 2 + share, LANES), BF16),
        in_specs=[pl.BlockSpec(memory_space=pltpu.VMEM)] * 2,
        out_specs=pl.BlockSpec(memory_space=pltpu.VMEM),
        compiler_params=pltpu.CompilerParams(vmem_limit_bytes=24 << 20),
        cost_estimate=pl.CostEstimate(
            flops=2 * rows * rows * nx * cols,
            bytes_accessed=4 * left.size + 2 * rows * rows,
            transcendentals=0,
        ),
    )(left, right)


def unpack_kernel(chunks, top, bottom):
    parts, half = chunks.shape[0], top.shape[0]
    share = chunks.shape[1] - half
    for part in range(parts):
        side, tile = (top, bottom)[part % 2], part // 2
        side[:, tile * LANES : (tile + 1) * LANES] = chunks[part, :half, :]
    last = parts // 2 * LANES
    for part in range(half // share):
        piece = chunks[part, half:, :]
        rows = slice(part * share, (part + 1) * share)
        top[rows, last:] = piece[:, : LANES // 2]
        bottom[rows, last:] = piece[:, LANES // 2 :]


def unpacked(chunks, rows, cols):
    half = jax.ShapeDtypeStruct((rows // 2, cols), BF16)
    return pl.pallas_call(
        unpack_kernel,
        out_shape=(half, half),
        in_specs=[pl.BlockSpec(memory_space=pltpu.VMEM)],
        out_specs=(pl.BlockSpec(memory_space=pltpu.VMEM),) * 2,
        compiler_params=pltpu.CompilerParams(vmem_limit_bytes=8 << 20),
        cost_estimate=pl.CostEstimate(
            flops=0, bytes_accessed=2 * chunks.size + 2 * rows * cols, transcendentals=0
        ),
    )(chunks)


def on_device(own):
    rows, cols = own.shape
    nx, ny, nz = (lax.axis_size(a) for a in "xyz")
    quarter = rows // nx
    depth = nz * quarter
    here = lax.axis_index("x")

    def shift_x(block, hop):
        return lax.ppermute(block, "x", [(i, (i + hop) % nx) for i in range(nx)])

    chunks = jnp.broadcast_to(own.reshape(nx, quarter, cols), (nz, nx, quarter, cols))
    chunks = exchange(chunks.reshape(nz * nx, quarter, cols), ("z", "x"))
    panel = by_column(chunks.reshape(nz, nx, quarter, cols))
    blocks = [own] + [shift_x(own, hop) for hop in range(1, nx)]
    order = [lax.rem(here + (nx - hop), nx) for hop in range(nx)]
    wide = jnp.stack([lax.select_n(hop, *blocks) for hop in order])

    left = jnp.concatenate([wide, swap_cores(wide)], 1)
    chunk = reduce_scatter(packed_gram(left, panel, ny), "y").astype(BF16)
    top, bottom = unpacked(gather(chunk, "y"), 2 * rows, depth)

    def times(left, right):
        return jnp.einsum("rj,xjc->xrc", left, right, preferred_element_type=F32)

    def applied(right):
        peer = swap_cores(times(bottom, right).astype(BF16))
        return lax.optimization_barrier(times(top, right)) + peer.astype(F32)

    first = reduce_scatter(applied(panel).astype(BF16), "x")
    inner = (-4.775 * own.astype(F32) + 2.0315 * first).astype(BF16).reshape(nx, quarter, cols)
    inner, top, bottom = lax.optimization_barrier((inner, top, bottom))
    right = by_column(gather(inner, "z"))
    above_top, below_bottom = shift_x(top, -1), shift_x(bottom, 1)
    above_bottom, below_top = shift_x(bottom, -1), shift_x(top, 1)
    far_top, far_bottom = shift_x(above_top, -1), shift_x(below_bottom, 1)
    bottoms = jnp.stack([bottom, below_bottom, far_bottom, above_bottom])
    other = swap_cores(product(bottoms, right))
    tops = jnp.stack([top, below_top, far_top, above_top])
    second = product(tops, right) + other
    scale = math.sqrt(COLS)
    return (scale * (3.4445 * own.astype(F32) + second)).astype(BF16)


def solution(mesh):
    fine = Mesh(mesh.devices.reshape(8, 2, 4, 8), ("z", "core", "x", "y"))
    placed = P(("z", "core"), ("x", "y"))
    return jax.shard_map(
        on_device, mesh=fine, in_specs=placed, out_specs=placed, check_vma=False
    )
```

```python
import math

import jax
import jax.numpy as jnp
from jax import lax
from jax.experimental import pallas as pl
from jax.experimental.pallas import tpu as pltpu
from jax.sharding import Mesh, PartitionSpec as P

COLS = 8192
F32, BF16 = jnp.float32, jnp.bfloat16


def exchange(chunks, axis):
    return lax.all_to_all(chunks, axis, 0, 0)


def gather(block, axis):
    return exchange(jnp.broadcast_to(block, (lax.axis_size(axis), *block.shape)), axis)


def reduce_scatter(chunks, axis):
    parts = exchange(chunks, axis)
    return sum(parts[i].astype(F32) for i in range(parts.shape[0]))


def swap_cores(block):
    return lax.ppermute(block, "core", [(0, 1), (1, 0)])


def by_column(blocks):
    n, nx, rows, cols = blocks.shape
    return blocks.swapaxes(0, 1).reshape(nx, n * rows, cols)


def product_kernel(right, *refs):
    *stacks, out = refs
    nx = right.shape[0]
    here = lax.axis_index("x")
    blocks = [stacks[0].at[hop] for hop in range(nx)] if len(stacks) == 1 else stacks
    out[...] = sum(
        jnp.dot(block[...], right[lax.rem(here + (nx - hop), nx)], preferred_element_type=F32)
        for hop, block in enumerate(blocks)
    )


def product(stacks, right):
    rows, cols = stacks[0].shape[-2], right.shape[2]
    size = sum(stack.size for stack in stacks)
    return pl.pallas_call(
        product_kernel,
        out_shape=jax.ShapeDtypeStruct((rows, cols), F32),
        in_specs=[pl.BlockSpec(memory_space=pltpu.VMEM)] * (1 + len(stacks)),
        out_specs=pl.BlockSpec(memory_space=pltpu.VMEM),
        compiler_params=pltpu.CompilerParams(vmem_limit_bytes=16 << 20),
        cost_estimate=pl.CostEstimate(
            flops=2 * size * cols,
            bytes_accessed=2 * right.size + 2 * size + 4 * rows * cols,
            transcendentals=0,
        ),
    )(right, *stacks)


LANES = 128


def gram_kernel(left, right, out):
    nx, rows, _ = left.shape
    total = sum(
        lax.dot_general(left[i], right[i], (((1,), (1,)), ((), ())), preferred_element_type=F32)
        for i in range(nx)
    ).astype(BF16)
    parts, half = out.shape[0], rows // 2
    share = out.shape[1] - half
    for part in range(parts):
        tile, side = part // 2, part % 2
        out[part, :half, :] = total[side * half : (side + 1) * half, tile * LANES : (tile + 1) * LANES]
    last = parts // 2 * LANES
    tail = jnp.concatenate([total[:half, last:], total[half:, last:]], 1)
    for part in range(parts):
        if part * share < half:
            out[part, half:, :] = tail[part * share : (part + 1) * share]
        else:
            out[part, half:, :] = jnp.zeros((share, LANES), BF16)


def packed_gram(left, right, parts):
    nx, rows, cols = left.shape
    share = 48
    return pl.pallas_call(
        gram_kernel,
        out_shape=jax.ShapeDtypeStruct((parts, rows // 2 + share, LANES), BF16),
        in_specs=[pl.BlockSpec(memory_space=pltpu.VMEM)] * 2,
        out_specs=pl.BlockSpec(memory_space=pltpu.VMEM),
        compiler_params=pltpu.CompilerParams(vmem_limit_bytes=24 << 20),
        cost_estimate=pl.CostEstimate(
            flops=2 * rows * rows * nx * cols,
            bytes_accessed=4 * left.size + 2 * rows * rows,
            transcendentals=0,
        ),
    )(left, right)


def unpack_kernel(chunks, top, bottom):
    parts, half = chunks.shape[0], top.shape[0]
    share = chunks.shape[1] - half
    for part in range(parts):
        side, tile = (top, bottom)[part % 2], part // 2
        side[:, tile * LANES : (tile + 1) * LANES] = chunks[part, :half, :]
    last = parts // 2 * LANES
    for part in range(half // share):
        piece = chunks[part, half:, :]
        rows = slice(part * share, (part + 1) * share)
        top[rows, last:] = piece[:, : LANES // 2]
        bottom[rows, last:] = piece[:, LANES // 2 :]


def unpacked(chunks, rows, cols):
    half = jax.ShapeDtypeStruct((rows // 2, cols), BF16)
    return pl.pallas_call(
        unpack_kernel,
        out_shape=(half, half),
        in_specs=[pl.BlockSpec(memory_space=pltpu.VMEM)],
        out_specs=(pl.BlockSpec(memory_space=pltpu.VMEM),) * 2,
        compiler_params=pltpu.CompilerParams(vmem_limit_bytes=8 << 20),
        cost_estimate=pl.CostEstimate(
            flops=0, bytes_accessed=2 * chunks.size + 2 * rows * cols, transcendentals=0
        ),
    )(chunks)


def on_device(own):
    rows, cols = own.shape
    nx, ny, nz = (lax.axis_size(a) for a in "xyz")
    quarter = rows // nx
    depth = nz * quarter
    here = lax.axis_index("x")

    def shift_x(block, hop):
        return lax.ppermute(block, "x", [(i, (i + hop) % nx) for i in range(nx)])

    chunks = jnp.broadcast_to(own.reshape(nx, quarter, cols), (nz, nx, quarter, cols))
    chunks = exchange(chunks.reshape(nz * nx, quarter, cols), ("z", "x"))
    panel = by_column(chunks.reshape(nz, nx, quarter, cols))
    blocks = [own] + [shift_x(own, hop) for hop in range(1, nx)]
    order = [lax.rem(here + (nx - hop), nx) for hop in range(nx)]
    wide = jnp.stack([lax.select_n(hop, *blocks) for hop in order])

    left = jnp.concatenate([wide, swap_cores(wide)], 1)
    chunk = reduce_scatter(packed_gram(left, panel, ny), "y").astype(BF16)
    top, bottom = unpacked(gather(chunk, "y"), 2 * rows, depth)

    def times(left, right):
        return jnp.einsum("rj,xjc->xrc", left, right, preferred_element_type=F32)

    def applied(right):
        peer = swap_cores(times(bottom, right).astype(BF16))
        return lax.optimization_barrier(times(top, right)) + peer.astype(F32)

    first = reduce_scatter(applied(panel).astype(BF16), "x")
    inner = (-4.775 * own.astype(F32) + 2.0315 * first).astype(BF16).reshape(nx, quarter, cols)
    inner, top, bottom = lax.optimization_barrier((inner, top, bottom))
    right = by_column(gather(inner, "z"))
    above_top, below_bottom = shift_x(top, -1), shift_x(bottom, 1)
    above_bottom, below_top = shift_x(bottom, -1), shift_x(top, 1)
    far_top, far_bottom = shift_x(above_top, -1), shift_x(below_bottom, 1)
    bottoms = jnp.stack([bottom, below_bottom, far_bottom, above_bottom])
    other = swap_cores(product((bottoms,), right))
    second = product((top, below_top, far_top, above_top), right) + other
    scale = math.sqrt(COLS)
    return (scale * (3.4445 * own.astype(F32) + second)).astype(BF16)


def solution(mesh):
    fine = Mesh(mesh.devices.reshape(8, 2, 4, 8), ("z", "core", "x", "y"))
    placed = P(("z", "core"), ("x", "y"))
    return jax.shard_map(
        on_device, mesh=fine, in_specs=placed, out_specs=placed, check_vma=False
    )
```
